32 devices in a mesh: dp: 8 (over z, x), head: 4 (over y, core).
Axes of the slice: x: 2, y: 2, z: 4, core: 2. Of those that a mesh axis runs over, the one named last changes fastest.
Arguments:
- grads: bfloat16 [8, 2, 512, 16384], P('dp', None, None, 'head'), may hold values from -6 to 6
- owners: int32 [2], replicated, may hold values from 0 to 7, as said below
Outputs:
- updates: bfloat16 [2, 512, 16384], P(None, 'dp', 'head')
- owned: bfloat16 [8, 512, 16384], P('dp', None, 'head')
The draws below stay inside these ranges and needn't reach their ends.
Inputs may be any that keep to these rules, and one draw needn't show every extreme that they name: The owners are distinct ranks of the data axis: each rank owns at most one of the 2 layers.
All inputs are finite; a program needn't handle non-finite values.
Results may differ from the reference program's by a relative error of at most 0.014.
Values may be sent and summed in bfloat16 or wider, within the bound.
A program may use at most 64 MiB of HBM per device.

```python
import math
import jax
import jax.numpy as jnp
from jax import lax

R = 512
HEADS = 64
HDIM = 256
LAYERS = 2
ITERS = 2
NCOL = 16384
N_DP = 8


def draw_owners(key, part):
    key = jax.random.fold_in(key, 7)
    return jax.random.permutation(key, N_DP)[:LAYERS].astype(jnp.int32)


def raised(entries, own_key, source, target, blocks, factor):
    owner, partner = [(jnp.arange(entries.shape[axis_at]) // (entries.shape[axis_at] // blocks)).reshape([-1 if axis == axis_at else 1 for axis in range(entries.ndim)]) for axis_at in (source, target)]
    chosen = jax.random.permutation(own_key, blocks)[partner]
    strong = (owner == chosen) | (owner == (partner + blocks // 2) % blocks)
    return jnp.where(strong, factor * entries, entries)


def block_scale(own_key, dims, pieces, low, high):
    def one(position, parts):
        steps = jax.random.uniform(jax.random.fold_in(jax.random.fold_in(own_key, 6), position), (parts,), jnp.float32, low / len(pieces), high / len(pieces))
        return jnp.repeat(jnp.exp(steps), dims[position] // parts).reshape((-1,) + (1,) * (len(dims) - position - 1))

    gain = one(*pieces[0])
    for cut in pieces[1:]:
        gain = gain * one(*cut)
    return gain


def bell_draw_with(rng, dims, deviation, limit, shards, heavy, kind=jnp.bfloat16):
    result = deviation * jax.random.normal(rng, dims, jnp.float32)
    if shards:
        result = result * block_scale(rng, dims, shards, -0.22, 0.18)
    return jnp.clip(raised(result, jax.random.fold_in(rng, 3), *heavy), -limit, limit).astype(kind)


def setup_inputs(seed: int = 0) -> dict:
    seeds = jax.random.split(jax.random.key(seed), 3)
    grads = bell_draw_with(seeds[0], (N_DP, LAYERS, R, NCOL), 1.0, 6.0, ((0, 8), (3, 4)), (0, 3, 8, 2.0))
    owners = draw_owners(jax.random.fold_in(seeds[2], 71), 0)
    return dict(grads=grads, owners=owners)


COEF_A = 3.4445
COEF_B = -4.775
COEF_C = 2.0315
EPS = 1e-07

def orthogonalize(start):
    iterate = start
    stepped = None
    for step_index in range(ITERS):
        gram_part = jnp.dot(iterate, iterate.T, preferred_element_type=jnp.float32)
        if step_index == 0:
            squares = jnp.trace(gram_part)
            inverse = lax.rsqrt(squares + EPS)
            gram = gram_part * (inverse * inverse)
        else:
            gram = gram_part
        polynomial = (COEF_B * gram + COEF_C * jnp.dot(gram, gram, precision=lax.Precision.HIGHEST)).astype(jnp.bfloat16)
        stepped = COEF_A * iterate.astype(jnp.float32) + jnp.dot(polynomial, iterate, preferred_element_type=jnp.float32)
        if step_index == 0:
            stepped = inverse * stepped
        if step_index + 1 < ITERS:
            iterate = stepped.astype(jnp.bfloat16)
    return stepped

def reference(grads, owners):

    def add_rank(total, partial_value):
        return (total + partial_value.astype(jnp.float32), None)
    total, _ = lax.scan(add_rank, jnp.zeros(grads.shape[1:], jnp.float32), grads)
    gsum = total.astype(jnp.bfloat16)
    factor = 0.2 * math.sqrt(max(R, HEADS * HDIM))
    updates = jnp.stack([(factor * orthogonalize(gsum[layer_index])).astype(jnp.bfloat16) for layer_index in range(LAYERS)])
    ranks = jnp.arange(N_DP, dtype=jnp.int32)
    is_owner = owners[None, :] == ranks[:, None]
    has_layer = jnp.any(is_owner, axis=1)
    chosen = jnp.argmax(is_owner.astype(jnp.int32), axis=1).astype(jnp.int32)
    owned = jnp.where(has_layer[:, None, None], updates[chosen], jnp.zeros((), jnp.bfloat16))
    return (updates, owned)
```

```python
import functools
import math

import jax
import jax.numpy as jnp
from jax import lax
from jax.experimental import pallas as pl
from jax.experimental.pallas import tpu as pltpu
from jax.sharding import PartitionSpec as P

COEF_A = 3.4445
COEF_B = -4.775
COEF_C = 2.0315
EPS = 1e-07
TILE = 512
START_ROUND = 5
MESH = pl.DeviceIdType.MESH
F32 = jnp.float32
BF16 = jnp.bfloat16


def add_rows(dst, terms, rows):
    step = 16

    @pl.loop(0, rows // step)
    def _(index):
        at = pl.ds(pl.multiple_of(index * step, step), step)
        total = terms[0][at, :].astype(F32)
        for term in terms[1:]:
            total = total + term[at, :].astype(F32)
        dst[at, :] = total.astype(BF16)


def remote(src, dst, send, recv, device):
    return pltpu.make_async_remote_copy(
        src_ref=src, dst_ref=dst, send_sem=send, recv_sem=recv, device_id=device, device_id_type=MESH
    )


class Line:
    def __init__(self, size, place, device):
        self.size, self.place, self.device = size, place, device

    def left(self):
        return self.device(self.place - 1)

    def right(self):
        return self.device(self.place + 1)


def reduce_scatter(line, view, out, rows, slots, send, recv, drain):
    n, i = line.size, line.place

    def receive(slot):
        remote(slots.at[slot], slots.at[slot], send.at[0, 0], recv.at[slot], line.device(i)).wait_recv()

    def rightward(t):
        copy = remote(view(t), slots.at[t], send.at[0, t], recv.at[t], line.right())
        if t > 1:
            @pl.when((i > 0) & (i < t))
            def _():
                receive(t)
                add_rows(view(t), [view(t), slots.at[t]], rows)

        pl.when(i < t)(copy.start)
        drain.append((i < t, copy))

    def leftward(t):
        slot = jnp.where(i - 1 == t, n, t)
        copy = remote(view(t), slots.at[slot], send.at[1, t], recv.at[slot], line.left())
        if t < n - 2:
            @pl.when((i > t) & (i < n - 1))
            def _():
                receive(t)
                add_rows(view(t), [view(t), slots.at[t]], rows)

        pl.when(i > t)(copy.start)
        drain.append((i > t, copy))

    for step in range(n - 1):
        rightward(n - 1 - step)
        yield
        leftward(step)
        yield

    @pl.when(i == 0)
    def _():
        receive(n)
        add_rows(out, [view(i), slots.at[n]], rows)

    @pl.when(i == n - 1)
    def _():
        receive(i)
        add_rows(out, [view(i), slots.at[i]], rows)

    if n > 2:
        @pl.when((i > 0) & (i < n - 1))
        def _():
            receive(i)
            receive(n)
            add_rows(out, [view(i), slots.at[i], slots.at[n]], rows)
    yield


def all_gather(line, view, send, recv, drain):
    n, i = line.size, line.place

    def move(way, step):
        t = i - step if way == 0 else i + step
        there = t >= 0 if way == 0 else t <= n - 1
        passes = there & (i < n - 1 if way == 0 else i > 0)
        target = line.right() if way == 0 else line.left()
        part = jnp.clip(t, 0, n - 1)
        copy = remote(view(part), view(part), send.at[way, step], recv.at[part], target)
        if step > 0:
            pl.when(there)(copy.wait_recv)
        if step < n - 1:
            pl.when(passes)(copy.start)
            drain.append((passes, copy))

    for step in range(n):
        move(0, step)
        move(1, step)
        yield


def spread_rows(index, rows):
    return pl.ds(pl.multiple_of(index * rows, rows), rows)


def kernel(sizes, *refs):
    z_size, x_size, y_size, rank, wide, wide_b, wide_total = sizes
    n_dp = z_size * x_size
    refs = list(refs)
    take = lambda count: [refs.pop(0) for _ in range(count)]
    grads, chosen, updates, owned = take(4)
    acc, fin = take(2), take(2)
    slots_a, slots_b = take(2), take(2)
    raw, half_in, by_y, full, m0, t0, g1, dmat, outs = take(9)
    load_sem = take(1)[0]
    rs_send, rs_recv = take(4), take(4)
    ag_send, ag_recv = take(4), take(4)
    core_send, core_recv, y_send, y_recv = take(4)

    me, head = lax.axis_index("dp"), lax.axis_index("head")
    z, x = me // x_size, me % x_size
    y, core = head // 2, head % 2
    line_x = Line(x_size, x, lambda place: (z * x_size + place, head))
    line_z = Line(z_size, z, lambda place: (place * x_size + x, head))
    sibling = (me, y * 2 + 1 - core)

    loads = {}
    for layer in range(2):
        for job, (start, width) in enumerate(((0, wide), (wide, wide_b))):
            loads[layer, job] = pltpu.make_async_copy(
                grads.at[0, layer, :, pl.ds(start, width)], acc[job].at[layer], load_sem.at[layer, job]
            )
            loads[layer, job].start()

    barrier = pltpu.get_barrier_semaphore()
    greet = [(z > 0, line_z.left()), (z < z_size - 1, line_z.right())]
    greet += [(x > 0, line_x.left()), (x < x_size - 1, line_x.right())]
    for near, device in greet:
        pl.when(near)(
            functools.partial(
                pl.semaphore_signal, barrier, inc=1, device_id=device, device_id_type=MESH
            )
        )
    pl.semaphore_signal(barrier, inc=1, device_id=sibling, device_id_type=MESH)
    peers = [(me, lax.rem(y + step, y_size) * 2 + core) for step in range(1, y_size)]
    for peer in peers:
        pl.semaphore_signal(barrier, inc=1, device_id=peer, device_id_type=MESH)
    count = jnp.int32(y_size)
    for near, _ in greet:
        count = count + near.astype(jnp.int32)
    pl.semaphore_wait(barrier, count)

    drain = []

    def chain(layer, job):
        first, second = (line_x, line_z) if job == 0 else (line_z, line_x)
        slots1, slots2 = slots_a if job == 0 else slots_b
        big, small = rank // first.size, rank // n_dp
        a, f = acc[job].at[layer], fin[job].at[layer]
        base = first.place * big

        def small_rows(t):
            return pl.ds(pl.multiple_of(base + t * small, small), small)

        loads[layer, job].wait()
        k = 2 * job
        yield from reduce_scatter(
            first, lambda t: a.at[spread_rows(t, big), :], a.at[spread_rows(first.place, big), :], big,
            slots1.at[layer], rs_send[k].at[layer], rs_recv[k].at[layer], drain,
        )
        yield from reduce_scatter(
            second, lambda t: a.at[small_rows(t), :], f.at[small_rows(second.place), :], small,
            slots2.at[layer], rs_send[k + 1].at[layer], rs_recv[k + 1].at[layer], drain,
        )
        yield from all_gather(
            second, lambda t: f.at[small_rows(t), :], ag_send[k + 1].at[layer], ag_recv[k + 1].at[layer], drain
        )
        yield from all_gather(
            first, lambda t: f.at[spread_rows(t, big), :], ag_send[k].at[layer], ag_recv[k].at[layer], drain
        )

    def gram_of(layer, job, width):
        @pl.loop(0, width // TILE)
        def _(index):
            block = fin[job][layer, :, pl.ds(pl.multiple_of(index * TILE, TILE), TILE)]
            raw[layer] += lax.dot_general(
                block, block, (((1,), (1,)), ((), ())), preferred_element_type=F32
            )

    def product(left, right, finish):
        step = 128

        @pl.loop(0, rank // step)
        def _(index):
            at = pl.ds(pl.multiple_of(index * step, step), step)
            finish(at, jnp.dot(left[at, :], right[...], precision=lax.Precision.HIGHEST,
                               preferred_element_type=F32), index * step)

    def eye(start):
        rows = lax.broadcasted_iota(jnp.int32, (128, rank), 0) + start
        return rows == lax.broadcasted_iota(jnp.int32, (128, rank), 1)

    def post(layer):
        raw[layer] = jnp.zeros((rank, rank), F32)
        gram_of(layer, 0, wide)
        yield
        gram_of(layer, 1, wide_b)
        half = rank // 2
        mine, other = spread_rows(core, half), spread_rows(1 - core, half)
        give = remote(raw.at[layer, other, :], half_in.at[layer], core_send.at[layer, 0],
                      core_recv.at[layer, 0], sibling)
        give.start()
        yield
        give.wait_recv()
        by_y[layer, y] = raw[layer, mine, :] + half_in[layer]
        sends = []
        for step, peer in enumerate(peers):
            copy = remote(by_y.at[layer, y], by_y.at[layer, y], y_send.at[layer, step],
                          y_recv.at[layer, y], peer)
            copy.start()
            sends.append(copy)
        yield
        yield
        for step in range(1, y_size):
            source = lax.rem(y + step, y_size)
            remote(by_y.at[layer, source], by_y.at[layer, source], y_send.at[layer, 0],
                   y_recv.at[layer, source], sibling).wait_recv()
        total = by_y[layer, 0]
        for place in range(1, y_size):
            total = total + by_y[layer, place]
        full[layer, mine, :] = total
        share = remote(full.at[layer, mine, :], full.at[layer, mine, :], core_send.at[layer, 1],
                       core_recv.at[layer, 1], sibling)
        share.start()
        give.wait_send()
        for copy in sends:
            copy.wait_send()
        yield
        share.wait_recv()
        share.wait_send()
        raws = full[layer]
        on_diagonal = lax.broadcasted_iota(jnp.int32, (rank, rank), 0) == lax.broadcasted_iota(
            jnp.int32, (rank, rank), 1)
        squares = jnp.sum(jnp.where(on_diagonal, raws, 0.0), axis=0, keepdims=True)
        squares = jnp.sum(squares, axis=1, keepdims=True)
        inverse = lax.rsqrt(squares + EPS)
        gram = raw.at[layer]
        gram[...] = raws * (inverse * inverse)

        def to_m0(at, value, start):
            m0[at, :] = COEF_B * gram[at, :] + COEF_C * value + jnp.where(eye(start), COEF_A, 0.0)

        product(gram, gram, to_m0)
        yield

        def to_t0(at, value, start):
            t0[at, :] = value

        product(m0, gram, to_t0)
        yield

        def to_g1(at, value, start):
            g1[at, :] = value

        product(t0, m0, to_g1)
        yield

        def to_m1(at, value, start):
            t0[at, :] = COEF_B * g1[at, :] + COEF_C * value

        product(g1, g1, to_m1)
        yield
        scale = inverse * (0.2 * math.sqrt(max(rank, wide_total)))

        def to_d(at, value, start):
            rest = value + COEF_A * (m0[at, :] - jnp.where(eye(start), COEF_A, 0.0))
            dmat[at, :] = (scale * rest).astype(BF16)

        product(t0, m0, to_d)
        yield
        weight = chosen[layer]
        rows = rank // n_dp
        diagonal = scale * (COEF_A * COEF_A)
        for job, (start, width) in enumerate(((0, wide), (wide, wide_b))):
            @pl.loop(0, width // TILE)
            def _(index):
                offset = pl.multiple_of(index * TILE, TILE)
                block = fin[job][layer, :, pl.ds(offset, TILE)]
                value = jnp.dot(dmat[...], block, preferred_element_type=F32)
                value = (value + diagonal * block.astype(F32)).astype(BF16)
                outs[...] = value
                at = pl.ds(pl.multiple_of(start + offset, TILE), TILE)
                updates[layer, :, at] = outs[spread_rows(me, rows), :]
                picked = weight * value.astype(F32)
                if layer > 0:
                    picked = picked + owned[0, :, at].astype(F32)
                owned[0, :, at] = picked.astype(BF16)

            yield

    def whole_layer(layer):
        waiting = [chain(layer, 0), chain(layer, 1)]
        while waiting:
            for job in list(waiting):
                if next(job, 0) == 0:
                    waiting.remove(job)
            yield
        yield from post(layer)

    flows = [whole_layer(0), whole_layer(1)]
    turn = 0
    while flows:
        for index, flow in enumerate(list(flows)):
            if len(flows) > 1 and index == 1 and turn < START_ROUND:
                continue
            if next(flow, 0) == 0:
                flows.remove(flow)
        turn += 1

    for sent, copy in drain:
        pl.when(sent)(copy.wait_send)


def per_device(mesh_shape, grads, owners):
    n_dp, n_head = mesh_shape["dp"], mesh_shape["head"]
    _, layers, rank, columns = grads.shape
    x_size = math.isqrt(n_dp // 2)
    z_size, y_size = n_dp // x_size, n_head // 2
    wide = max(TILE, columns * 5 // 8 // TILE * TILE)
    wide_b = columns - wide
    chosen = (owners == lax.axis_index("dp")).astype(F32)
    dma = pltpu.SemaphoreType.DMA

    def slots(first, width):
        second = n_dp // first
        return [
            pltpu.VMEM((layers, first + 1, rank // first, width), BF16),
            pltpu.VMEM((layers, second + 1, rank // n_dp, width), BF16),
        ]

    order = (x_size, z_size, z_size, x_size)
    square = pltpu.VMEM((rank, rank), F32)
    pair = pltpu.VMEM((layers, rank, rank), F32)
    flat = [pltpu.VMEM((layers, rank, w), BF16) for w in (wide, wide_b)]
    scratch = flat + flat + slots(x_size, wide) + slots(z_size, wide_b)
    scratch += [
        pair,
        pltpu.VMEM((layers, rank // 2, rank), F32),
        pltpu.VMEM((layers, y_size, rank // 2, rank), F32),
        pair, square, square, square,
        pltpu.VMEM((rank, rank), BF16),
        pltpu.VMEM((rank, TILE), BF16),
        dma((layers, 2)),
    ]
    scratch += [dma((layers, 2, n)) for n in order] + [dma((layers, n + 1)) for n in order]
    scratch += [dma((layers, 2, n)) for n in order] + [dma((layers, n)) for n in order]
    scratch += [dma((layers, 2)), dma((layers, 2)), dma((layers, y_size)), dma((layers, y_size))]
    vmem = pl.BlockSpec(memory_space=pltpu.VMEM)
    return pl.pallas_call(
        functools.partial(kernel, (z_size, x_size, y_size, rank, wide, wide_b, columns * n_head)),
        out_shape=(
            jax.ShapeDtypeStruct((layers, rank // n_dp, columns), BF16),
            jax.ShapeDtypeStruct((1, rank, columns), BF16),
        ),
        in_specs=[pl.BlockSpec(memory_space=pl.ANY), pl.BlockSpec(memory_space=pltpu.SMEM)],
        out_specs=(vmem, vmem),
        scratch_shapes=scratch,
        compiler_params=pltpu.CompilerParams(
            collective_id=0, has_side_effects=True, vmem_limit_bytes=58 * 1024 * 1024
        ),
    )(grads, chosen)


def solution(mesh):
    in_specs = (P("dp", None, None, "head"), P())
    out_specs = (P(None, "dp", "head"), P("dp", None, "head"))
    return jax.shard_map(
        functools.partial(per_device, dict(mesh.shape)),
        mesh=mesh, in_specs=in_specs, out_specs=out_specs, check_vma=False,
    )
```

```python
import functools
import math

import jax
import jax.numpy as jnp
from jax import lax
from jax.experimental import pallas as pl
from jax.experimental.pallas import tpu as pltpu
from jax.sharding import PartitionSpec as P

COEF_A = 3.4445
COEF_B = -4.775
COEF_C = 2.0315
EPS = 1e-07
TILE = 512
START_ROUND = 5
MESH = pl.DeviceIdType.MESH
F32 = jnp.float32
BF16 = jnp.bfloat16


def add_rows(dst, terms, rows):
    step = 16

    @pl.loop(0, rows // step)
    def _(index):
        at = pl.ds(pl.multiple_of(index * step, step), step)
        total = terms[0][at, :].astype(F32)
        for term in terms[1:]:
            total = total + term[at, :].astype(F32)
        dst[at, :] = total.astype(BF16)


def remote(src, dst, send, recv, device):
    return pltpu.make_async_remote_copy(
        src_ref=src, dst_ref=dst, send_sem=send, recv_sem=recv, device_id=device, device_id_type=MESH
    )


class Line:
    def __init__(self, size, place, device):
        self.size, self.place, self.device = size, place, device

    def left(self):
        return self.device(self.place - 1)

    def right(self):
        return self.device(self.place + 1)


def reduce_scatter(line, view, out, rows, slots, send, recv, drain):
    n, i = line.size, line.place

    def receive(slot):
        remote(slots.at[slot], slots.at[slot], send.at[0, 0], recv.at[slot], line.device(i)).wait_recv()

    def rightward(t):
        copy = remote(view(t), slots.at[t], send.at[0, t], recv.at[t], line.right())
        if t > 1:
            @pl.when((i > 0) & (i < t))
            def _():
                receive(t)
                add_rows(view(t), [view(t), slots.at[t]], rows)

        pl.when(i < t)(copy.start)
        drain.append((i < t, copy))

    def leftward(t):
        slot = jnp.where(i - 1 == t, n, t)
        copy = remote(view(t), slots.at[slot], send.at[1, t], recv.at[slot], line.left())
        if t < n - 2:
            @pl.when((i > t) & (i < n - 1))
            def _():
                receive(t)
                add_rows(view(t), [view(t), slots.at[t]], rows)

        pl.when(i > t)(copy.start)
        drain.append((i > t, copy))

    for step in range(n - 1):
        rightward(n - 1 - step)
        yield
        leftward(step)
        yield

    @pl.when(i == 0)
    def _():
        receive(n)
        add_rows(out, [view(i), slots.at[n]], rows)

    @pl.when(i == n - 1)
    def _():
        receive(i)
        add_rows(out, [view(i), slots.at[i]], rows)

    if n > 2:
        @pl.when((i > 0) & (i < n - 1))
        def _():
            receive(i)
            receive(n)
            add_rows(out, [view(i), slots.at[i], slots.at[n]], rows)
    yield


def all_gather(line, view, send, recv, drain):
    n, i = line.size, line.place

    def move(way, step):
        t = i - step if way == 0 else i + step
        there = t >= 0 if way == 0 else t <= n - 1
        passes = there & (i < n - 1 if way == 0 else i > 0)
        target = line.right() if way == 0 else line.left()
        part = jnp.clip(t, 0, n - 1)
        copy = remote(view(part), view(part), send.at[way, step], recv.at[part], target)
        if step > 0:
            pl.when(there)(copy.wait_recv)
        if step < n - 1:
            pl.when(passes)(copy.start)
            drain.append((passes, copy))

    for step in range(n):
        move(0, step)
        move(1, step)
        yield


def spread_rows(index, rows):
    return pl.ds(pl.multiple_of(index * rows, rows), rows)


def kernel(sizes, *refs):
    z_size, x_size, y_size, rank, wide, wide_b, wide_total = sizes
    n_dp = z_size * x_size
    refs = list(refs)
    take = lambda count: [refs.pop(0) for _ in range(count)]
    grads, chosen, updates, owned = take(4)
    acc, fin = take(2), take(2)
    slots_a, slots_b = take(2), take(2)
    raw, half_in, by_y, full, m0, t0, g1, dmat, outs, right_hi, right_lo = take(11)
    load_sem = take(1)[0]
    rs_send, rs_recv = take(4), take(4)
    ag_send, ag_recv = take(4), take(4)
    core_send, core_recv, y_send, y_recv = take(4)

    me, head = lax.axis_index("dp"), lax.axis_index("head")
    z, x = me // x_size, me % x_size
    y, core = head // 2, head % 2
    line_x = Line(x_size, x, lambda place: (z * x_size + place, head))
    line_z = Line(z_size, z, lambda place: (place * x_size + x, head))
    sibling = (me, y * 2 + 1 - core)

    loads = {}
    for layer in range(2):
        for job, (start, width) in enumerate(((0, wide), (wide, wide_b))):
            loads[layer, job] = pltpu.make_async_copy(
                grads.at[0, layer, :, pl.ds(start, width)], acc[job].at[layer], load_sem.at[layer, job]
            )
            loads[layer, job].start()

    barrier = pltpu.get_barrier_semaphore()
    greet = [(z > 0, line_z.left()), (z < z_size - 1, line_z.right())]
    greet += [(x > 0, line_x.left()), (x < x_size - 1, line_x.right())]
    for near, device in greet:
        pl.when(near)(
            functools.partial(
                pl.semaphore_signal, barrier, inc=1, device_id=device, device_id_type=MESH
            )
        )
    pl.semaphore_signal(barrier, inc=1, device_id=sibling, device_id_type=MESH)
    peers = [(me, lax.rem(y + step, y_size) * 2 + core) for step in range(1, y_size)]
    for peer in peers:
        pl.semaphore_signal(barrier, inc=1, device_id=peer, device_id_type=MESH)
    count = jnp.int32(y_size)
    for near, _ in greet:
        count = count + near.astype(jnp.int32)
    pl.semaphore_wait(barrier, count)

    drain = []

    def chain(layer, job):
        first, second = (line_x, line_z) if job == 0 else (line_z, line_x)
        slots1, slots2 = slots_a if job == 0 else slots_b
        big, small = rank // first.size, rank // n_dp
        a, f = acc[job].at[layer], fin[job].at[layer]
        base = first.place * big

        def small_rows(t):
            return pl.ds(pl.multiple_of(base + t * small, small), small)

        loads[layer, job].wait()
        k = 2 * job
        yield from reduce_scatter(
            first, lambda t: a.at[spread_rows(t, big), :], a.at[spread_rows(first.place, big), :], big,
            slots1.at[layer], rs_send[k].at[layer], rs_recv[k].at[layer], drain,
        )
        yield from reduce_scatter(
            second, lambda t: a.at[small_rows(t), :], f.at[small_rows(second.place), :], small,
            slots2.at[layer], rs_send[k + 1].at[layer], rs_recv[k + 1].at[layer], drain,
        )
        yield from all_gather(
            second, lambda t: f.at[small_rows(t), :], ag_send[k + 1].at[layer], ag_recv[k + 1].at[layer], drain
        )
        yield from all_gather(
            first, lambda t: f.at[spread_rows(t, big), :], ag_send[k].at[layer], ag_recv[k].at[layer], drain
        )

    def gram_of(layer, job, width):
        @pl.loop(0, width // TILE)
        def _(index):
            block = fin[job][layer, :, pl.ds(pl.multiple_of(index * TILE, TILE), TILE)]
            raw[layer] += lax.dot_general(
                block, block, (((1,), (1,)), ((), ())), preferred_element_type=F32
            )

    def product(left, right, finish):
        step = 256
        value = right[...]
        right_hi[...] = value.astype(BF16)
        right_lo[...] = (value - right_hi[...].astype(F32)).astype(BF16)

        @pl.loop(0, rank // step)
        def _(index):
            at = pl.ds(pl.multiple_of(index * step, step), step)
            block = left[at, :]
            hi = block.astype(BF16)
            lo = (block - hi.astype(F32)).astype(BF16)
            dot = functools.partial(jnp.dot, preferred_element_type=F32)
            total = dot(hi, right_lo[...]) + dot(lo, right_hi[...]) + dot(hi, right_hi[...])
            finish(at, total, index * step)

    def eye(start):
        rows = lax.broadcasted_iota(jnp.int32, (256, rank), 0) + start
        return rows == lax.broadcasted_iota(jnp.int32, (256, rank), 1)

    def post(layer):
        raw[layer] = jnp.zeros((rank, rank), F32)
        gram_of(layer, 0, wide)
        yield
        gram_of(layer, 1, wide_b)
        half = rank // 2
        mine, other = spread_rows(core, half), spread_rows(1 - core, half)
        give = remote(raw.at[layer, other, :], half_in.at[layer], core_send.at[layer, 0],
                      core_recv.at[layer, 0], sibling)
        give.start()
        yield
        give.wait_recv()
        by_y[layer, y] = (raw[layer, mine, :] + half_in[layer]).astype(BF16)
        sends = []
        for step, peer in enumerate(peers):
            copy = remote(by_y.at[layer, y], by_y.at[layer, y], y_send.at[layer, step],
                          y_recv.at[layer, y], peer)
            copy.start()
            sends.append(copy)
        yield
        yield
        for step in range(1, y_size):
            source = lax.rem(y + step, y_size)
            remote(by_y.at[layer, source], by_y.at[layer, source], y_send.at[layer, 0],
                   y_recv.at[layer, source], sibling).wait_recv()
        total = by_y[layer, 0].astype(F32)
        for place in range(1, y_size):
            total = total + by_y[layer, place].astype(F32)
        full[layer, mine, :] = total
        share = remote(full.at[layer, mine, :], full.at[layer, mine, :], core_send.at[layer, 1],
                       core_recv.at[layer, 1], sibling)
        share.start()
        give.wait_send()
        for copy in sends:
            copy.wait_send()
        yield
        share.wait_recv()
        share.wait_send()
        raws = full[layer]
        on_diagonal = lax.broadcasted_iota(jnp.int32, (rank, rank), 0) == lax.broadcasted_iota(
            jnp.int32, (rank, rank), 1)
        squares = jnp.sum(jnp.where(on_diagonal, raws, 0.0), axis=0, keepdims=True)
        squares = jnp.sum(squares, axis=1, keepdims=True)
        inverse = lax.rsqrt(squares + EPS)
        gram = raw.at[layer]
        gram[...] = raws * (inverse * inverse)

        def to_m0(at, value, start):
            m0[at, :] = COEF_B * gram[at, :] + COEF_C * value + jnp.where(eye(start), COEF_A, 0.0)

        product(gram, gram, to_m0)
        yield

        def to_t0(at, value, start):
            t0[at, :] = value

        product(m0, gram, to_t0)
        yield

        def to_g1(at, value, start):
            g1[at, :] = value

        product(t0, m0, to_g1)
        yield

        def to_m1(at, value, start):
            t0[at, :] = COEF_B * g1[at, :] + COEF_C * value

        product(g1, g1, to_m1)
        yield
        scale = inverse * (0.2 * math.sqrt(max(rank, wide_total)))

        def to_d(at, value, start):
            rest = value + COEF_A * (m0[at, :] - jnp.where(eye(start), COEF_A, 0.0))
            dmat[at, :] = (scale * rest).astype(BF16)

        product(t0, m0, to_d)
        yield
        weight = chosen[layer]
        rows = rank // n_dp
        diagonal = scale * (COEF_A * COEF_A)
        for job, (start, width) in enumerate(((0, wide), (wide, wide_b))):
            @pl.loop(0, width // TILE)
            def _(index):
                offset = pl.multiple_of(index * TILE, TILE)
                block = fin[job][layer, :, pl.ds(offset, TILE)]
                value = jnp.dot(dmat[...], block, preferred_element_type=F32)
                value = (value + diagonal * block.astype(F32)).astype(BF16)
                outs[...] = value
                at = pl.ds(pl.multiple_of(start + offset, TILE), TILE)
                updates[layer, :, at] = outs[spread_rows(me, rows), :]
                picked = weight * value.astype(F32)
                if layer > 0:
                    picked = picked + owned[0, :, at].astype(F32)
                owned[0, :, at] = picked.astype(BF16)

            yield

    def whole_layer(layer):
        waiting = [chain(layer, 0), chain(layer, 1)]
        while waiting:
            for job in list(waiting):
                if next(job, 0) == 0:
                    waiting.remove(job)
            yield
        yield from post(layer)

    flows = [whole_layer(0), whole_layer(1)]
    turn = 0
    while flows:
        for index, flow in enumerate(list(flows)):
            if len(flows) > 1 and index == 1 and turn < START_ROUND:
                continue
            if next(flow, 0) == 0:
                flows.remove(flow)
        turn += 1

    for sent, copy in drain:
        pl.when(sent)(copy.wait_send)


def per_device(mesh_shape, grads, owners):
    n_dp, n_head = mesh_shape["dp"], mesh_shape["head"]
    _, layers, rank, columns = grads.shape
    x_size = math.isqrt(n_dp // 2)
    z_size, y_size = n_dp // x_size, n_head // 2
    wide = max(TILE, columns * 5 // 8 // TILE * TILE)
    wide_b = columns - wide
    chosen = (owners == lax.axis_index("dp")).astype(F32)
    dma = pltpu.SemaphoreType.DMA

    def slots(first, width):
        second = n_dp // first
        return [
            pltpu.VMEM((layers, first + 1, rank // first, width), BF16),
            pltpu.VMEM((layers, second + 1, rank // n_dp, width), BF16),
        ]

    order = (x_size, z_size, z_size, x_size)
    square = pltpu.VMEM((rank, rank), F32)
    pair = pltpu.VMEM((layers, rank, rank), F32)
    flat = [pltpu.VMEM((layers, rank, w), BF16) for w in (wide, wide_b)]
    scratch = flat + flat + slots(x_size, wide) + slots(z_size, wide_b)
    scratch += [
        pair,
        pltpu.VMEM((layers, rank // 2, rank), F32),
        pltpu.VMEM((layers, y_size, rank // 2, rank), BF16),
        pair, square, square, square,
        pltpu.VMEM((rank, rank), BF16),
        pltpu.VMEM((rank, TILE), BF16),
        pltpu.VMEM((rank, rank), BF16), pltpu.VMEM((rank, rank), BF16),
        dma((layers, 2)),
    ]
    scratch += [dma((layers, 2, n)) for n in order] + [dma((layers, n + 1)) for n in order]
    scratch += [dma((layers, 2, n)) for n in order] + [dma((layers, n)) for n in order]
    scratch += [dma((layers, 2)), dma((layers, 2)), dma((layers, y_size)), dma((layers, y_size))]
    vmem = pl.BlockSpec(memory_space=pltpu.VMEM)
    return pl.pallas_call(
        functools.partial(kernel, (z_size, x_size, y_size, rank, wide, wide_b, columns * n_head)),
        out_shape=(
            jax.ShapeDtypeStruct((layers, rank // n_dp, columns), BF16),
            jax.ShapeDtypeStruct((1, rank, columns), BF16),
        ),
        in_specs=[pl.BlockSpec(memory_space=pl.ANY), pl.BlockSpec(memory_space=pltpu.SMEM)],
        out_specs=(vmem, vmem),
        scratch_shapes=scratch,
        compiler_params=pltpu.CompilerParams(
            collective_id=0, has_side_effects=True, vmem_limit_bytes=58 * 1024 * 1024
        ),
    )(grads, chosen)


def solution(mesh):
    in_specs = (P("dp", None, None, "head"), P())
    out_specs = (P(None, "dp", "head"), P("dp", None, "head"))
    return jax.shard_map(
        functools.partial(per_device, dict(mesh.shape)),
        mesh=mesh, in_specs=in_specs, out_specs=out_specs, check_vma=False,
    )
```

```python
import functools
import math

import jax
import jax.numpy as jnp
from jax import lax
from jax.experimental import pallas as pl
from jax.experimental.pallas import tpu as pltpu
from jax.sharding import PartitionSpec as P

COEF_A = 3.4445
COEF_B = -4.775
COEF_C = 2.0315
EPS = 1e-07
TILE = 512
START_ROUND = 4
MESH = pl.DeviceIdType.MESH
F32 = jnp.float32
BF16 = jnp.bfloat16


def add_rows(dst, terms, rows):
    step = 16

    @pl.loop(0, rows // step)
    def _(index):
        at = pl.ds(pl.multiple_of(index * step, step), step)
        total = terms[0][at, :].astype(F32)
        for term in terms[1:]:
            total = total + term[at, :].astype(F32)
        dst[at, :] = total.astype(BF16)


def remote(src, dst, send, recv, device):
    return pltpu.make_async_remote_copy(
        src_ref=src, dst_ref=dst, send_sem=send, recv_sem=recv, device_id=device, device_id_type=MESH
    )


class Line:
    def __init__(self, size, place, device):
        self.size, self.place, self.device = size, place, device

    def left(self):
        return self.device(self.place - 1)

    def right(self):
        return self.device(self.place + 1)


def reduce_scatter(line, view, out, rows, slots, send, recv, drain, pause=0):
    n, i = line.size, line.place

    def receive(slot):
        remote(slots.at[slot], slots.at[slot], send.at[0, 0], recv.at[slot], line.device(i)).wait_recv()

    def rightward(t):
        copy = remote(view(t), slots.at[t], send.at[0, t], recv.at[t], line.right())
        if t > 1:
            @pl.when((i > 0) & (i < t))
            def _():
                receive(t)
                add_rows(view(t), [view(t), slots.at[t]], rows)

        pl.when(i < t)(copy.start)
        drain.append((i < t, copy))

    def leftward(t):
        slot = jnp.where(i - 1 == t, n, t)
        copy = remote(view(t), slots.at[slot], send.at[1, t], recv.at[slot], line.left())
        if t < n - 2:
            @pl.when((i > t) & (i < n - 1))
            def _():
                receive(t)
                add_rows(view(t), [view(t), slots.at[t]], rows)

        pl.when(i > t)(copy.start)
        drain.append((i > t, copy))

    for step in range(n - 1):
        rightward(n - 1 - step)
        yield
        leftward(step)
        yield

    for _ in range(pause):
        yield

    @pl.when(i == 0)
    def _():
        receive(n)
        add_rows(out, [view(i), slots.at[n]], rows)

    @pl.when(i == n - 1)
    def _():
        receive(i)
        add_rows(out, [view(i), slots.at[i]], rows)

    if n > 2:
        @pl.when((i > 0) & (i < n - 1))
        def _():
            receive(i)
            receive(n)
            add_rows(out, [view(i), slots.at[i], slots.at[n]], rows)
    yield


def all_gather(line, view, send, recv, drain):
    n, i = line.size, line.place

    def move(way, step):
        t = i - step if way == 0 else i + step
        there = t >= 0 if way == 0 else t <= n - 1
        passes = there & (i < n - 1 if way == 0 else i > 0)
        target = line.right() if way == 0 else line.left()
        part = jnp.clip(t, 0, n - 1)
        copy = remote(view(part), view(part), send.at[way, step], recv.at[part], target)
        if step > 0:
            pl.when(there)(copy.wait_recv)
        if step < n - 1:
            pl.when(passes)(copy.start)
            drain.append((passes, copy))

    for step in range(n):
        move(0, step)
        move(1, step)
        yield


def spread_rows(index, rows):
    return pl.ds(pl.multiple_of(index * rows, rows), rows)


def kernel(sizes, *refs):
    z_size, x_size, y_size, rank, wide, wide_b, wide_total = sizes
    n_dp = z_size * x_size
    refs = list(refs)
    take = lambda count: [refs.pop(0) for _ in range(count)]
    grads, chosen, updates, owned = take(4)
    acc, fin = take(2), take(2)
    slots_a, slots_b = take(2), take(2)
    raw, half_in, by_y, full, m0, t0, g1, dmat, outs, right_hi, right_lo = take(11)
    load_sem = take(1)[0]
    rs_send, rs_recv = take(4), take(4)
    ag_send, ag_recv = take(4), take(4)
    core_send, core_recv, y_send, y_recv = take(4)

    me, head = lax.axis_index("dp"), lax.axis_index("head")
    z, x = me // x_size, me % x_size
    y, core = head // 2, head % 2
    line_x = Line(x_size, x, lambda place: (z * x_size + place, head))
    line_z = Line(z_size, z, lambda place: (place * x_size + x, head))
    sibling = (me, y * 2 + 1 - core)

    loads = {}
    for layer in range(2):
        for job, (start, width) in enumerate(((0, wide), (wide, wide_b))):
            loads[layer, job] = pltpu.make_async_copy(
                grads.at[0, layer, :, pl.ds(start, width)], acc[job].at[layer], load_sem.at[layer, job]
            )
            loads[layer, job].start()

    barrier = pltpu.get_barrier_semaphore()
    greet = [(z > 0, line_z.left()), (z < z_size - 1, line_z.right())]
    greet += [(x > 0, line_x.left()), (x < x_size - 1, line_x.right())]
    for near, device in greet:
        pl.when(near)(
            functools.partial(
                pl.semaphore_signal, barrier, inc=1, device_id=device, device_id_type=MESH
            )
        )
    pl.semaphore_signal(barrier, inc=1, device_id=sibling, device_id_type=MESH)
    peers = [(me, lax.rem(y + step, y_size) * 2 + core) for step in range(1, y_size)]
    for peer in peers:
        pl.semaphore_signal(barrier, inc=1, device_id=peer, device_id_type=MESH)
    count = jnp.int32(y_size)
    for near, _ in greet:
        count = count + near.astype(jnp.int32)
    pl.semaphore_wait(barrier, count)

    drain = []

    def chain(layer, job):
        first, second = (line_x, line_z) if job == 0 else (line_z, line_x)
        slots1, slots2 = slots_a if job == 0 else slots_b
        big, small = rank // first.size, rank // n_dp
        a, f = acc[job].at[layer], fin[job].at[layer]
        base = first.place * big

        def small_rows(t):
            return pl.ds(pl.multiple_of(base + t * small, small), small)

        loads[layer, job].wait()
        k = 2 * job
        yield from reduce_scatter(
            first, lambda t: a.at[spread_rows(t, big), :], a.at[spread_rows(first.place, big), :], big,
            slots1.at[layer], rs_send[k].at[layer], rs_recv[k].at[layer], drain, 3 if layer > 0 and job == 0 else 0,
        )
        yield from reduce_scatter(
            second, lambda t: a.at[small_rows(t), :], f.at[small_rows(second.place), :], small,
            slots2.at[layer], rs_send[k + 1].at[layer], rs_recv[k + 1].at[layer], drain,
        )
        yield from all_gather(
            second, lambda t: f.at[small_rows(t), :], ag_send[k + 1].at[layer], ag_recv[k + 1].at[layer], drain
        )
        yield from all_gather(
            first, lambda t: f.at[spread_rows(t, big), :], ag_send[k].at[layer], ag_recv[k].at[layer], drain
        )

    def gram_of(layer, job, width):
        @pl.loop(0, width // TILE)
        def _(index):
            block = fin[job][layer, :, pl.ds(pl.multiple_of(index * TILE, TILE), TILE)]
            raw[layer] += lax.dot_general(
                block, block, (((1,), (1,)), ((), ())), preferred_element_type=F32
            )

    def product(left, right, finish):
        step = 256
        value = right[...]
        right_hi[...] = value.astype(BF16)
        right_lo[...] = (value - right_hi[...].astype(F32)).astype(BF16)

        @pl.loop(0, rank // step)
        def _(index):
            at = pl.ds(pl.multiple_of(index * step, step), step)
            block = left[at, :]
            hi = block.astype(BF16)
            lo = (block - hi.astype(F32)).astype(BF16)
            dot = functools.partial(jnp.dot, preferred_element_type=F32)
            total = dot(hi, right_lo[...]) + dot(lo, right_hi[...]) + dot(hi, right_hi[...])
            finish(at, total, index * step)

    def eye(start):
        rows = lax.broadcasted_iota(jnp.int32, (256, rank), 0) + start
        return rows == lax.broadcasted_iota(jnp.int32, (256, rank), 1)

    def post(layer):
        raw[layer] = jnp.zeros((rank, rank), F32)
        gram_of(layer, 0, wide)
        yield
        gram_of(layer, 1, wide_b)
        half = rank // 2
        mine, other = spread_rows(core, half), spread_rows(1 - core, half)
        give = remote(raw.at[layer, other, :], half_in.at[layer], core_send.at[layer, 0],
                      core_recv.at[layer, 0], sibling)
        give.start()
        yield
        give.wait_recv()
        by_y[layer, y] = (raw[layer, mine, :] + half_in[layer]).astype(BF16)
        sends = []
        for step, peer in enumerate(peers):
            copy = remote(by_y.at[layer, y], by_y.at[layer, y], y_send.at[layer, step],
                          y_recv.at[layer, y], peer)
            copy.start()
            sends.append(copy)
        yield
        yield
        for step in range(1, y_size):
            source = lax.rem(y + step, y_size)
            remote(by_y.at[layer, source], by_y.at[layer, source], y_send.at[layer, 0],
                   y_recv.at[layer, source], sibling).wait_recv()
        total = by_y[layer, 0].astype(F32)
        for place in range(1, y_size):
            total = total + by_y[layer, place].astype(F32)
        full[layer, mine, :] = total
        share = remote(full.at[layer, mine, :], full.at[layer, mine, :], core_send.at[layer, 1],
                       core_recv.at[layer, 1], sibling)
        share.start()
        give.wait_send()
        for copy in sends:
            copy.wait_send()
        yield
        share.wait_recv()
        share.wait_send()
        raws = full[layer]
        on_diagonal = lax.broadcasted_iota(jnp.int32, (rank, rank), 0) == lax.broadcasted_iota(
            jnp.int32, (rank, rank), 1)
        squares = jnp.sum(jnp.where(on_diagonal, raws, 0.0), axis=0, keepdims=True)
        squares = jnp.sum(squares, axis=1, keepdims=True)
        inverse = lax.rsqrt(squares + EPS)
        gram = raw.at[layer]
        gram[...] = raws * (inverse * inverse)

        def to_m0(at, value, start):
            m0[at, :] = COEF_B * gram[at, :] + COEF_C * value + jnp.where(eye(start), COEF_A, 0.0)

        product(gram, gram, to_m0)
        yield

        def to_t0(at, value, start):
            t0[at, :] = value

        product(m0, gram, to_t0)
        yield

        def to_g1(at, value, start):
            g1[at, :] = value

        product(t0, m0, to_g1)
        yield

        def to_m1(at, value, start):
            t0[at, :] = COEF_B * g1[at, :] + COEF_C * value

        product(g1, g1, to_m1)
        yield
        scale = inverse * (0.2 * math.sqrt(max(rank, wide_total)))

        def to_d(at, value, start):
            rest = value + COEF_A * (m0[at, :] - jnp.where(eye(start), COEF_A, 0.0))
            dmat[at, :] = (scale * rest).astype(BF16)

        product(t0, m0, to_d)
        yield
        weight = chosen[layer]
        rows = rank // n_dp
        diagonal = scale * (COEF_A * COEF_A)
        for job, (start, width) in enumerate(((0, wide), (wide, wide_b))):
            @pl.loop(0, width // TILE)
            def _(index):
                offset = pl.multiple_of(index * TILE, TILE)
                block = fin[job][layer, :, pl.ds(offset, TILE)]
                value = jnp.dot(dmat[...], block, preferred_element_type=F32)
                value = (value + diagonal * block.astype(F32)).astype(BF16)
                outs[...] = value
                at = pl.ds(pl.multiple_of(start + offset, TILE), TILE)
                updates[layer, :, at] = outs[spread_rows(me, rows), :]
                picked = weight * value.astype(F32)
                if layer > 0:
                    picked = picked + owned[0, :, at].astype(F32)
                owned[0, :, at] = picked.astype(BF16)

            yield

    def whole_layer(layer):
        waiting = [chain(layer, 0), chain(layer, 1)]
        while waiting:
            for job in list(waiting):
                if next(job, 0) == 0:
                    waiting.remove(job)
            yield
        yield from post(layer)

    flows = [whole_layer(0), whole_layer(1)]
    turn = 0
    while flows:
        for index, flow in enumerate(list(flows)):
            if len(flows) > 1 and index == 1 and turn < START_ROUND:
                continue
            if next(flow, 0) == 0:
                flows.remove(flow)
        turn += 1

    for sent, copy in drain:
        pl.when(sent)(copy.wait_send)


def per_device(mesh_shape, grads, owners):
    n_dp, n_head = mesh_shape["dp"], mesh_shape["head"]
    _, layers, rank, columns = grads.shape
    x_size = math.isqrt(n_dp // 2)
    z_size, y_size = n_dp // x_size, n_head // 2
    wide = max(TILE, columns * 5 // 8 // TILE * TILE)
    wide_b = columns - wide
    chosen = (owners == lax.axis_index("dp")).astype(F32)
    dma = pltpu.SemaphoreType.DMA

    def slots(first, width):
        second = n_dp // first
        return [
            pltpu.VMEM((layers, first + 1, rank // first, width), BF16),
            pltpu.VMEM((layers, second + 1, rank // n_dp, width), BF16),
        ]

    order = (x_size, z_size, z_size, x_size)
    square = pltpu.VMEM((rank, rank), F32)
    pair = pltpu.VMEM((layers, rank, rank), F32)
    flat = [pltpu.VMEM((layers, rank, w), BF16) for w in (wide, wide_b)]
    scratch = flat + flat + slots(x_size, wide) + slots(z_size, wide_b)
    scratch += [
        pair,
        pltpu.VMEM((layers, rank // 2, rank), F32),
        pltpu.VMEM((layers, y_size, rank // 2, rank), BF16),
        pair, square, square, square,
        pltpu.VMEM((rank, rank), BF16),
        pltpu.VMEM((rank, TILE), BF16),
        pltpu.VMEM((rank, rank), BF16), pltpu.VMEM((rank, rank), BF16),
        dma((layers, 2)),
    ]
    scratch += [dma((layers, 2, n)) for n in order] + [dma((layers, n + 1)) for n in order]
    scratch += [dma((layers, 2, n)) for n in order] + [dma((layers, n)) for n in order]
    scratch += [dma((layers, 2)), dma((layers, 2)), dma((layers, y_size)), dma((layers, y_size))]
    vmem = pl.BlockSpec(memory_space=pltpu.VMEM)
    return pl.pallas_call(
        functools.partial(kernel, (z_size, x_size, y_size, rank, wide, wide_b, columns * n_head)),
        out_shape=(
            jax.ShapeDtypeStruct((layers, rank // n_dp, columns), BF16),
            jax.ShapeDtypeStruct((1, rank, columns), BF16),
        ),
        in_specs=[pl.BlockSpec(memory_space=pl.ANY), pl.BlockSpec(memory_space=pltpu.SMEM)],
        out_specs=(vmem, vmem),
        scratch_shapes=scratch,
        compiler_params=pltpu.CompilerParams(
            collective_id=0, has_side_effects=True, vmem_limit_bytes=58 * 1024 * 1024
        ),
    )(grads, chosen)


def solution(mesh):
    in_specs = (P("dp", None, None, "head"), P())
    out_specs = (P(None, "dp", "head"), P("dp", None, "head"))
    return jax.shard_map(
        functools.partial(per_device, dict(mesh.shape)),
        mesh=mesh, in_specs=in_specs, out_specs=out_specs, check_vma=False,
    )
```
